32 devices in a mesh: lat: 4 (over x, core), lon: 8 (over z, y).
Axes of the slice: x: 2, y: 2, z: 4, core: 2. Of those that a mesh axis runs over, the one named last changes fastest.
Arguments:
- prior_ensemble: bfloat16 [3, 128, 8, 1024], P(None, None, 'lat', 'lon'), may hold values from -6 to 6
- observed: float32 [4, 8, 256], P('lat', 'lon'), may hold values from -6 to 6
- obs_error: float32 [4, 8, 256], P('lat', 'lon'), may hold values from 0.2 to 80
- obs_index: int32 [4, 8, 256], P('lat', 'lon'), may hold values from 0 to 767
- obs_count: int32 [4, 8], P('lat', 'lon'), may hold values from 128 to 256, as said below
Outputs:
- posterior_ensemble: float32 [3, 128, 8, 1024], P(None, None, 'lat', 'lon')
The draws below stay inside these ranges and needn't reach their ends.
Inputs may be any that keep to these rules, and one draw needn't show every extreme that they name: `obs_count`: every tile has between 128 and 256 live slots; some tile has all 256.
All inputs are finite; a program needn't handle non-finite values.
Results may differ from the reference program's by a relative error of at most 0.0003.
Values sent between devices are 32-bit elements; how exact they have to be, the bound alone decides.
A program may use at most 128 MiB of HBM per device.

```python
import math
import jax
import jax.numpy as jnp
from jax import lax

ENSEMBLE_SIZE = 128
NOBS = 256
CLAT = 2
CLON = 128
NLAT = 8
NLON = 1024
N_LAT = 4
N_LON = 8


def draw_obs_error(key, part):
    tile_key, row_key = jax.random.split(jax.random.fold_in(key, 11))
    tile_scale = jnp.exp(jax.random.uniform(tile_key, (N_LAT, N_LON, 1), jnp.float32, math.log(0.1), math.log(10.0)))
    row_scale = jnp.exp(jax.random.uniform(row_key, (N_LAT, N_LON, NOBS), jnp.float32, 0.0, math.log(4.0)))
    return 2.0 * tile_scale * row_scale


def draw_obs_count(key, part):
    counts = jax.random.randint(jax.random.fold_in(key, 23), (N_LAT, N_LON), NOBS // 2, NOBS + 1)
    counts = counts.at[0, 0].set(NOBS)
    counts = counts.at[N_LAT - 1, N_LON - 1].set(NOBS // 2)
    return counts.astype(jnp.int32)


def place_ends(array, rng, smallest, high):
    place = [jax.random.randint(jax.random.fold_in(rng, axis), (), 0, length) for axis, length in enumerate(array.shape)]
    widest = array.shape.index(max(array.shape))
    neighbour = place[:widest] + [(place[widest] + 1) % array.shape[widest]] + place[widest + 1:]
    return array.at[tuple(place)].set(smallest).at[tuple(neighbour)].set(high)


def level_of(stream_key, dims, cuts, smallest, top_value):
    loudness, own = 1.0, jax.random.fold_in(stream_key, 6)
    for axis_at, shards_of in cuts:
        steps = jnp.exp(jax.random.uniform(jax.random.fold_in(own, axis_at), (shards_of,), jnp.float32, smallest / len(cuts), top_value / len(cuts)))
        loudness = loudness * jnp.repeat(steps, dims[axis_at] // shards_of).reshape([-1 if axis == axis_at else 1 for axis in range(len(dims))])
    return loudness


def scatter_about(rng, shape, width, limit, shards=(), kind=jnp.bfloat16):
    array = jax.random.normal(rng, shape, jnp.float32) * width
    if len(shards) > 0:
        array = level_of(rng, shape, shards, -0.22, 0.18) * array
    return jnp.clip(array, min=-limit, max=limit).astype(kind)


def setup_inputs(seed: int = 0) -> dict:
    key_list = jax.random.split(jax.random.key(seed), 6)
    prior_ensemble = scatter_about(key_list[0], (3, ENSEMBLE_SIZE, NLAT, NLON), 1.0, 6.0, ((2, 4), (3, 8)))
    observed = scatter_about(key_list[1], (N_LAT, N_LON, NOBS), 1.0, 6.0, ((0, 4), (1, 8)), jnp.float32)
    obs_error = draw_obs_error(jax.random.fold_in(key_list[5], 71), 0)
    obs_index = place_ends(jax.random.randint(key_list[3], (N_LAT, N_LON, NOBS), 0, 3 * CLAT * CLON), jax.random.fold_in(key_list[3], 1), 0, (3 * CLAT * CLON) - 1).astype(jnp.int32)
    obs_count = draw_obs_count(jax.random.fold_in(key_list[5], 71), 0)
    return {"prior_ensemble": prior_ensemble, "observed": observed, "obs_error": obs_error, "obs_index": obs_index, "obs_count": obs_count}


HALF_COURANT = 0.4
ROTATION = 0.8
BAND = math.pi / 6.0

def rotation_rows(first_row, count, total_rows):
    rows = first_row + jnp.arange(count, dtype=jnp.int32)
    latitude = BAND * (2.0 * (rows.astype(jnp.float32) + 0.5) / total_rows - 1.0)
    return (ROTATION * jnp.sin(latitude))[:, None]

def tendency(padded, rotation):
    height, zonal_wind, merid_wind = (padded[0], padded[1], padded[2])
    d_height = -HALF_COURANT * (zonal_wind[..., 1:-1, 2:] - zonal_wind[..., 1:-1, :-2] + (merid_wind[..., 2:, 1:-1] - merid_wind[..., :-2, 1:-1]))
    d_zonal = -HALF_COURANT * (height[..., 1:-1, 2:] - height[..., 1:-1, :-2]) + rotation * merid_wind[..., 1:-1, 1:-1]
    d_merid = -HALF_COURANT * (height[..., 2:, 1:-1] - height[..., :-2, 1:-1]) - rotation * zonal_wind[..., 1:-1, 1:-1]
    return jnp.stack([d_height, d_zonal, d_merid], axis=0)

def wrap_pad(system_vector):
    padded = jnp.pad(system_vector, ((0, 0), (1, 1), (0, 0)))
    return jnp.concatenate([padded[..., -1:], padded, padded[..., :1]], axis=-1)

def reference(prior_ensemble, observed, obs_error, obs_index, obs_count):
    total_rows = CLAT * N_LAT
    rotation = rotation_rows(0, total_rows, total_rows)

    def advance_time(member):
        system_vector = member.astype(jnp.float32)
        upper_coefficient = tendency(wrap_pad(system_vector), rotation)
        midpoint = system_vector + upper_coefficient
        lower_coefficient = tendency(wrap_pad(midpoint), rotation)
        return system_vector + 0.5 * (upper_coefficient + lower_coefficient)
    predicted_ensemble = jnp.moveaxis(lax.map(advance_time, jnp.moveaxis(prior_ensemble, 1, 0)), 0, 1)
    mesh_points = CLAT * CLON
    tile_lat = jnp.arange(N_LAT, dtype=jnp.int32)[:, None, None]
    tile_lon = jnp.arange(N_LON, dtype=jnp.int32)[None, :, None]
    variable_slot = obs_index // mesh_points
    cell_index = obs_index % mesh_points
    latitude_slot = tile_lat * CLAT + cell_index // CLON
    longitude_slot = tile_lon * CLON + cell_index % CLON
    measured_vector = predicted_ensemble[variable_slot, :, latitude_slot, longitude_slot]
    state_mean = lax.optimization_barrier(jnp.mean(measured_vector, axis=-1))
    live = (jnp.arange(NOBS, dtype=jnp.int32)[None, None, :] < obs_count[:, :, None]).astype(jnp.float32)
    weight_rows = live / obs_error
    scaled = ((measured_vector - state_mean[..., None]) * weight_rows[..., None]).reshape(-1, ENSEMBLE_SIZE)
    innovation = ((observed - state_mean) * weight_rows).reshape(-1)
    gram = jnp.dot(scaled.T, scaled, precision=lax.Precision.HIGHEST)
    push = jnp.dot(innovation, scaled, precision=lax.Precision.HIGHEST)
    identity = jnp.eye(ENSEMBLE_SIZE, dtype=jnp.float32)
    prior = float(ENSEMBLE_SIZE - 1)
    factor = jnp.linalg.cholesky(prior * identity + gram)
    inverse = lax.linalg.triangular_solve(factor, identity, left_side=True, lower=True)
    transform = math.sqrt(prior) * inverse.T
    forward = lax.linalg.triangular_solve(factor, push[:, None], left_side=True, lower=True)
    mean_weights = lax.linalg.triangular_solve(factor, forward, left_side=True, lower=True, transpose_a=True)
    weights = transform + mean_weights
    unrolled_vector = predicted_ensemble.reshape(3, ENSEMBLE_SIZE, -1)
    state_center = lax.optimization_barrier(jnp.mean(unrolled_vector, axis=1, keepdims=True))
    anomaly = unrolled_vector - state_center
    posterior_ensemble = state_center + jnp.einsum('fic,ij->fjc', anomaly, weights, precision=lax.Precision.HIGHEST)
    return posterior_ensemble.reshape(predicted_ensemble.shape)
```

```python
import functools
import math

import jax
import jax.numpy as jnp
from jax import lax
from jax.experimental import pallas as pl
from jax.experimental.pallas import tpu as pltpu
from jax.sharding import PartitionSpec as P

HALF_COURANT = 0.4
ROTATION = 0.8
BAND = math.pi / 6.0
MESH = pl.DeviceIdType.MESH
F32 = jnp.float32
BF16 = jnp.bfloat16
HIGHEST = lax.Precision.HIGHEST
NT = (((1,), (1,)), ((), ()))
TN = (((0,), (0,)), ((), ()))
PANEL = 8


def split3(value):
    high = value.astype(BF16).astype(F32)
    rest = value - high
    middle = rest.astype(BF16).astype(F32)
    return high, middle, rest - middle


def forecast_kernel(
    n_lat, n_lon, prior, observed, obs_error, obs_index, obs_count,
    fields_out, total_out,
    wide, own, up_buf, down_buf, edges, from_low, from_high, cols, part, gathered, whole,
    send_sem, recv_sem, part_send, part_recv, whole_send, whole_recv,
):
    members = own.shape[1]
    lanes = own.shape[2]
    total = n_lat * n_lon
    lat = lax.axis_index("lat")
    lon = lax.axis_index("lon")
    me = lat * n_lon + lon
    east = lax.rem(lon + 1, n_lon)
    west = lax.rem(lon + n_lon - 1, n_lon)
    has_low = lat > 0
    has_high = lat < n_lat - 1
    chunks = part.shape[0]

    def place(index):
        return (index // n_lon, lax.rem(index, n_lon))

    def owner(chunk):
        line = 2 * (chunk // n_lon)
        return (line % n_lat + line // n_lat) * n_lon + chunk % n_lon

    barrier = pltpu.get_barrier_semaphore()

    def greet(step, carry):
        pl.semaphore_signal(
            barrier, inc=1, device_id=place(lax.rem(me + step, total)), device_id_type=MESH
        )
        return carry

    lax.fori_loop(1, total, greet, 0)

    wide[...] = prior[...].astype(F32)
    field_at = {"h": 0, "u": 1, "v": 2}
    slot_of = {"h": 0, "v": 1, "u": 2}
    state = {}
    for row in range(2):
        for name in "huv":
            block = wide[pl.ds(field_at[name] * 2 * members + row, members, stride=2), :]
            state[name, row] = block
            own[row * 3 + slot_of[name]] = block

    pick_row = lax.broadcasted_iota(jnp.int32, (8, lanes), 0)
    pick_col = lax.broadcasted_iota(jnp.int32, (8, lanes), 1)
    wanted = jnp.where(pick_row < 2, pick_row, pick_row + (lanes - 4))
    picker = jnp.where((pick_col == wanted) & (pick_row < 4), 1.0, 0.0).astype(BF16)
    for row in range(2):
        for at, name in enumerate("huv"):
            start = (row * 3 + at) * 8
            edges[start : start + 8, :] = lax.dot_general(
                picker, state[name, row].astype(BF16), NT, preferred_element_type=F32
            )

    lane = lax.broadcasted_iota(jnp.int32, (members, lanes), 1)
    first = lane == 0
    last = lane == lanes - 1
    zero = jnp.zeros((members, lanes), F32)

    def span(value, halo):
        ahead = jnp.where(last, halo, pltpu.roll(value, lanes - 1, 1))
        behind = jnp.where(first, halo, pltpu.roll(value, 1, 1))
        return ahead - behind

    rows = lat * 2 + lax.broadcasted_iota(jnp.int32, (8, lanes), 0)
    latitude = BAND * (2.0 * (rows.astype(F32) + 0.5) / (2 * n_lat) - 1.0)
    rotation = ROTATION * jnp.sin(latitude)
    rot = [rotation[row : row + 1, :] for row in range(2)]

    @pl.when(jnp.logical_not(has_low))
    def _():
        from_low[...] = jnp.zeros_like(from_low)
        cols[96:128, :] = jnp.zeros((32, members), F32)

    @pl.when(jnp.logical_not(has_high))
    def _():
        from_high[...] = jnp.zeros_like(from_high)
        cols[128:160, :] = jnp.zeros((32, members), F32)

    pl.semaphore_wait(barrier, total - 1)

    def copy(source, target, at, to):
        return pltpu.make_async_remote_copy(
            src_ref=source, dst_ref=target, send_sem=send_sem.at[at], recv_sem=recv_sem.at[at],
            device_id=to, device_id_type=MESH,
        )

    def rows_of(buf, start, count):
        return buf.at[pl.ds(start, count)]

    lon_copies = [
        copy(edges, rows_of(cols, 48, 48), 0, (lat, west)),
        copy(edges, rows_of(cols, 0, 48), 1, (lat, east)),
    ]
    low = lat - 1
    high = lat + 1
    low_copies = [
        copy(rows_of(own, 0, 2), rows_of(from_high, 0, 2), 2, (low, lon)),
        copy(down_buf, rows_of(from_high, 2, 2), 3, (low, lon)),
        copy(rows_of(edges, 8, 16), rows_of(cols, 144, 16), 4, (low, west)),
        copy(rows_of(edges, 8, 16), rows_of(cols, 128, 16), 5, (low, east)),
    ]
    high_copies = [
        copy(rows_of(own, 3, 2), rows_of(from_low, 0, 2), 6, (high, lon)),
        copy(up_buf, rows_of(from_low, 2, 2), 7, (high, lon)),
        copy(rows_of(edges, 32, 16), rows_of(cols, 112, 16), 8, (high, west)),
        copy(rows_of(edges, 32, 16), rows_of(cols, 96, 16), 9, (high, east)),
    ]

    @pl.when(has_high)
    def _():
        high_copies[0].start()

    @pl.when(has_low)
    def _():
        low_copies[0].start()

    for item in lon_copies:
        item.start()

    h0, u0, v0 = (state[name, 0] for name in "huv")
    h1, u1, v1 = (state[name, 1] for name in "huv")
    c = HALF_COURANT
    up_buf[0] = h1 - c * span(u1, zero) + c * v0
    up_buf[1] = v1 + c * h0 - rot[1] * u1
    down_buf[0] = h0 - c * span(u0, zero) - c * v1
    down_buf[1] = v0 - c * h1 - rot[0] * u0

    @pl.when(has_high)
    def _():
        for item in high_copies[1:]:
            item.start()

    @pl.when(has_low)
    def _():
        for item in low_copies[1:]:
            item.start()

    slots = observed.shape[1]
    slot = lax.broadcasted_iota(jnp.int32, (1, slots), 1)
    live = jnp.where(slot < obs_count[0, 0], 1.0, 0.0)
    scale = live / obs_error[...]
    squared = scale * scale
    pieces = split3(squared) + split3(squared * observed[...])
    pieces = jnp.concatenate(pieces + (jnp.zeros((2, slots), F32),), axis=0).astype(BF16)
    cells = 6 * lanes
    cell = lax.broadcasted_iota(jnp.int32, (cells, slots), 0)
    hits = jnp.where(cell == obs_index[...], 1.0, 0.0).astype(BF16)
    sums = lax.dot_general(pieces, hits, NT, preferred_element_type=F32)
    weight = sums[0:1] + sums[1:2] + sums[2:3]
    target = sums[3:4] + sums[4:5] + sums[5:6]

    for item in lon_copies:
        item.wait()

    @pl.when(has_high)
    def _():
        for item in high_copies:
            item.wait_send()
        for item in low_copies:
            item.wait_recv()

    @pl.when(has_low)
    def _():
        for item in low_copies:
            item.wait_send()
        for item in high_copies:
            item.wait_recv()

    ahead_t = cols[...].astype(BF16)
    key = lax.broadcasted_iota(jnp.int32, (160, lanes), 0)
    spot = lax.broadcasted_iota(jnp.int32, (160, lanes), 1)

    def halo(west_at, east_at):
        chosen = jnp.where(
            ((key == west_at) & (spot == 0)) | ((key == east_at) & (spot == lanes - 1)), 1.0, 0.0
        ).astype(BF16)
        return lax.dot_general(ahead_t, chosen, TN, preferred_element_type=F32)

    def near(name, row):
        if 0 <= row < 2:
            at = (row * 3 + "huv".index(name)) * 8
            return halo(at + 3, 48 + at)
        base = 96 if row < 0 else 128
        at = base + "uv".index(name) * 8
        return halo(at + 3, at + 16)

    def far(name, row):
        at = (row * 3 + "huv".index(name)) * 8
        return halo(at + 2, 48 + at + 1)

    side = jnp.where(first, -1.0, jnp.where(last, 1.0, 0.0))
    inside_low = jnp.where(has_low, 1.0, 0.0)
    inside_high = jnp.where(has_high, 1.0, 0.0)

    hm, vm, pm, qm = (from_low[at] for at in range(4))
    hp, vp, pp, qp = (from_high[at] for at in range(4))
    mid_h = {
        -1: pm - c * side * near("u", -1) - (c * inside_low) * v0,
        2: pp - c * side * near("u", 2) + (c * inside_high) * v1,
    }
    mid_v = {-1: qm - (c * inside_low) * h0, 2: qp + (c * inside_high) * h1}
    h = {-1: hm, 0: h0, 1: h1, 2: hp}
    v = {-1: vm, 0: v0, 1: v1, 2: vp}
    u = {0: u0, 1: u1}
    near_v = {row: near("v", row) for row in range(-1, 3)}
    rate = {}
    mid_u = {}
    edge_h = {}
    edge_u = {}
    for row in range(2):
        near_u = near("u", row)
        near_h = near("h", row)
        rate["h", row] = -c * (span(u[row], near_u) + (v[row + 1] - v[row - 1]))
        rate["u", row] = -c * span(h[row], near_h) + rot[row] * v[row]
        rate["v", row] = -c * (h[row + 1] - h[row - 1]) - rot[row] * u[row]
        mid_h[row] = h[row] + rate["h", row]
        mid_u[row] = u[row] + rate["u", row]
        mid_v[row] = v[row] + rate["v", row]
        edge_h[row] = near_h - c * (
            side * (far("u", row) - u[row]) + (near_v[row + 1] - near_v[row - 1])
        )
        edge_u[row] = near_u - c * side * (far("h", row) - h[row]) + rot[row] * near_v[row]

    centered = []
    shifts = []
    for at, name in enumerate("huv"):
        for row in range(2):
            if name == "h":
                second = -c * (span(mid_u[row], edge_u[row]) + (mid_v[row + 1] - mid_v[row - 1]))
            elif name == "u":
                second = -c * span(mid_h[row], edge_h[row]) + rot[row] * mid_v[row]
            else:
                second = -c * (mid_h[row + 1] - mid_h[row - 1]) - rot[row] * mid_u[row]
            value = state[name, row] + 0.5 * (rate[name, row] + second)
            center = jnp.sum(value, axis=0, keepdims=True) * (1.0 / members)
            block = slice((at * 2 + row) * lanes, (at * 2 + row + 1) * lanes)
            fields_out[0:members, block] = value - center
            fields_out[members : members + 8, block] = jnp.broadcast_to(center, (8, lanes))

    anomaly = fields_out[0:members, :]
    center = fields_out[members : members + 1, :]
    bottom = jnp.broadcast_to(target - weight * center, (8, cells))
    left = jnp.concatenate([anomaly * weight, bottom], axis=0)
    local = lax.dot_general(left, anomaly, NT, precision=HIGHEST, preferred_element_type=F32)
    for chunk in range(chunks):
        part[chunk] = local[chunk * 8 : chunk * 8 + 8, :]

    def part_copy(chunk):
        target_device = owner(chunk)
        distance = lax.rem(me - target_device + total, total)
        return pltpu.make_async_remote_copy(
            src_ref=part.at[chunk], dst_ref=gathered.at[distance - 1],
            send_sem=part_send.at[chunk], recv_sem=part_recv,
            device_id=place(target_device), device_id_type=MESH,
        )

    for chunk in range(chunks):
        @pl.when(owner(chunk) != me)
        def _():
            part_copy(chunk).start()

    def whole_copy(chunk, step):
        return pltpu.make_async_remote_copy(
            src_ref=whole.at[chunk], dst_ref=whole.at[chunk],
            send_sem=whole_send, recv_sem=whole_recv.at[chunk],
            device_id=place(lax.rem(me + step, total)), device_id_type=MESH,
        )

    for chunk in range(chunks):
        @pl.when(owner(chunk) == me)
        def _():
            pltpu.make_async_copy(gathered, gathered, part_recv).wait()
            whole[chunk] = part[chunk] + jnp.sum(gathered[...], axis=0)

            def send(step, carry):
                whole_copy(chunk, step).start()
                return carry

            lax.fori_loop(1, total, send, 0)

    for chunk in range(chunks):
        @pl.when(owner(chunk) != me)
        def _():
            part_copy(chunk).wait_send()
            whole_copy(chunk, 1).wait_recv()

        total_out[chunk * 8 : chunk * 8 + 8, :] = whole[chunk]

    for chunk in range(chunks):
        @pl.when(owner(chunk) == me)
        def _():
            pltpu.make_async_copy(gathered, gathered, whole_send).wait()


def update_kernel(fields, sums, out, work, inverse):
    members = work.shape[0]
    lanes = out.shape[1]
    prior = float(members - 1)
    row = lax.broadcasted_iota(jnp.int32, (members, members), 0)
    col = lax.broadcasted_iota(jnp.int32, (members, members), 1)
    work[...] = sums[0:members, :] + jnp.where(row == col, prior, 0.0)
    sub = lax.broadcasted_iota(jnp.int32, (PANEL, members), 0)
    at = lax.broadcasted_iota(jnp.int32, (PANEL, members), 1)
    for start in range(0, members, PANEL):
        stop = start + PANEL
        panel = work[start:stop, :]
        columns = [
            jnp.broadcast_to(panel[:, start + k : start + k + 1], (PANEL, members))
            for k in range(PANEL)
        ]
        reciprocal = jnp.zeros((PANEL, members), F32)
        for k in range(PANEL):
            over = 1.0 / columns[k][k : k + 1, :]
            reciprocal = jnp.where(sub == k, over, reciprocal)
            ratio = jnp.where(sub > k, columns[k] * over, 0.0)
            panel = jnp.where(at == start + k, jnp.where(sub == k, 1.0, jnp.where(sub > k, 0.0, panel)), panel)
            panel = panel - ratio * panel[k : k + 1, :]
            for j in range(k + 1, PANEL):
                columns[j] = columns[j] - ratio * columns[j][k : k + 1, :]
        inverse[start:stop, :] = jnp.where(at <= start + sub, panel, 0.0) * jnp.sqrt(reciprocal)
        if stop < members:
            ratios = panel * reciprocal
            used = jnp.where((at > start + sub) & (at < stop), 0.0, panel)
            change = lax.dot_general(
                ratios, used, TN, precision=HIGHEST, preferred_element_type=F32
            )
            below = work[stop:, :]
            keep = (col[stop:, :] < start) | (col[stop:, :] >= stop)
            work[stop:, :] = jnp.where(keep, below, 0.0) - change[stop:, :]
    lower = inverse[...]
    push = sums[members : members + 8, :]
    forward = lax.dot_general(push, lower, NT, precision=HIGHEST, preferred_element_type=F32)
    mean_weights = jnp.dot(forward, lower, precision=HIGHEST, preferred_element_type=F32)
    weights = math.sqrt(prior) * lower + mean_weights[0:1, :]
    anomaly = fields[0:members, :]
    center = fields[members : members + 1, :]
    result = center + jnp.dot(weights, anomaly, precision=HIGHEST, preferred_element_type=F32)
    for block in range(6):
        field, line = block // 2, block % 2
        out[pl.ds(field * 2 * members + line, members, stride=2), :] = result[
            :, block * lanes : (block + 1) * lanes
        ]


def shards(n_lat, n_lon, prior_ensemble, observed, obs_error, obs_index, obs_count):
    fields, members, rows, lanes = prior_ensemble.shape
    cells = fields * rows * lanes
    total = n_lat * n_lon
    chunks = members // 8 + 1
    vmem = pl.BlockSpec(memory_space=pltpu.VMEM)
    smem = pl.BlockSpec(memory_space=pltpu.SMEM)
    slots = observed.shape[-1]
    forecast, sums = pl.pallas_call(
        functools.partial(forecast_kernel, n_lat, n_lon),
        out_shape=(
            jax.ShapeDtypeStruct((members + 8, cells), F32),
            jax.ShapeDtypeStruct((members + 8, members), F32),
        ),
        in_specs=[vmem, vmem, vmem, vmem, smem],
        out_specs=(vmem, vmem),
        scratch_shapes=[
            pltpu.VMEM((fields * members * rows, lanes), F32),
            pltpu.VMEM((6, members, lanes), F32),
            pltpu.VMEM((2, members, lanes), F32),
            pltpu.VMEM((2, members, lanes), F32),
            pltpu.VMEM((48, members), F32),
            pltpu.VMEM((4, members, lanes), F32),
            pltpu.VMEM((4, members, lanes), F32),
            pltpu.VMEM((160, members), F32),
            pltpu.VMEM((chunks, 8, members), F32),
            pltpu.VMEM((total - 1, 8, members), F32),
            pltpu.VMEM((chunks, 8, members), F32),
            pltpu.SemaphoreType.DMA((10,)),
            pltpu.SemaphoreType.DMA((10,)),
            pltpu.SemaphoreType.DMA((chunks,)),
            pltpu.SemaphoreType.DMA,
            pltpu.SemaphoreType.DMA,
            pltpu.SemaphoreType.DMA((chunks,)),
        ],
        compiler_params=pltpu.CompilerParams(
            collective_id=0, has_side_effects=True, vmem_limit_bytes=32 * 1024 * 1024
        ),
    )(
        prior_ensemble.reshape(-1, lanes), observed.reshape(1, slots), obs_error.reshape(1, slots),
        obs_index.reshape(1, slots), obs_count,
    )
    out = pl.pallas_call(
        update_kernel,
        out_shape=jax.ShapeDtypeStruct((fields * members * rows, lanes), F32),
        in_specs=[vmem, vmem],
        out_specs=vmem,
        scratch_shapes=[
            pltpu.VMEM((members, members), F32),
            pltpu.VMEM((members, members), F32),
        ],
        compiler_params=pltpu.CompilerParams(vmem_limit_bytes=32 * 1024 * 1024),
    )(forecast, sums)
    return out.reshape(prior_ensemble.shape)


def solution(mesh):
    placed = (
        P(None, None, "lat", "lon"),
        P("lat", "lon", None),
        P("lat", "lon", None),
        P("lat", "lon", None),
        P("lat", "lon"),
    )
    return jax.shard_map(
        functools.partial(shards, mesh.shape["lat"], mesh.shape["lon"]),
        mesh=mesh, in_specs=placed, out_specs=P(None, None, "lat", "lon"), check_vma=False,
    )
```

```python
import functools
import math

import jax
import jax.numpy as jnp
from jax import lax
from jax.experimental import pallas as pl
from jax.experimental.pallas import tpu as pltpu
from jax.sharding import PartitionSpec as P

HALF_COURANT = 0.4
ROTATION = 0.8
BAND = math.pi / 6.0
MESH = pl.DeviceIdType.MESH
F32 = jnp.float32
BF16 = jnp.bfloat16
HIGHEST = lax.Precision.HIGHEST
NT = (((1,), (1,)), ((), ()))
TN = (((0,), (0,)), ((), ()))
PANEL = 16
VMEM_LIMIT = 56 * 1024 * 1024


def split3(value):
    high = value.astype(BF16).astype(F32)
    rest = value - high
    middle = rest.astype(BF16).astype(F32)
    return high, middle, rest - middle


def forecast_kernel(
    n_lat, n_lon, prior_in, observed_in, obs_error_in, obs_index_in, count_in,
    fields_out, total_out,
    prior, observed, obs_error, obs_index, obs_count, in_sem,
    wide, own, up_buf, down_buf, edges, from_low, from_high, cols, part, gathered, whole,
    send_sem, recv_sem, part_send, part_recv, whole_send, whole_recv,
):
    members = own.shape[1]
    lanes = own.shape[2]
    total = n_lat * n_lon
    lat = lax.axis_index("lat")
    lon = lax.axis_index("lon")
    me = lat * n_lon + lon
    east = lax.rem(lon + 1, n_lon)
    west = lax.rem(lon + n_lon - 1, n_lon)
    has_low = lat > 0
    has_high = lat < n_lat - 1
    chunks = part.shape[0]

    def place(index):
        return (index // n_lon, lax.rem(index, n_lon))

    def owner(chunk):
        line = 2 * (chunk // n_lon)
        return (line % n_lat + line // n_lat) * n_lon + chunk % n_lon

    fetches = [
        pltpu.make_async_copy(source, target, in_sem.at[at])
        for at, (source, target) in enumerate(
            (
                (prior_in, prior), (observed_in, observed), (obs_error_in, obs_error),
                (obs_index_in, obs_index), (count_in, obs_count),
            )
        )
    ]
    for item in fetches:
        item.start()
    barrier = pltpu.get_barrier_semaphore()

    def greet(step, carry):
        pl.semaphore_signal(
            barrier, inc=1, device_id=place(lax.rem(me + step, total)), device_id_type=MESH
        )
        return carry

    lax.fori_loop(1, total, greet, 0)
    fetches[0].wait()

    wide[...] = prior[...].astype(F32)
    field_at = {"h": 0, "u": 1, "v": 2}
    slot_of = {"h": 0, "v": 1, "u": 2}
    state = {}
    for row in range(2):
        for name in "huv":
            block = wide[pl.ds(field_at[name] * 2 * members + row, members, stride=2), :]
            state[name, row] = block
            own[row * 3 + slot_of[name]] = block

    pick_row = lax.broadcasted_iota(jnp.int32, (8, lanes), 0)
    pick_col = lax.broadcasted_iota(jnp.int32, (8, lanes), 1)
    wanted = jnp.where(pick_row < 2, pick_row, pick_row + (lanes - 4))
    picker = jnp.where((pick_col == wanted) & (pick_row < 4), 1.0, 0.0).astype(BF16)
    for row in range(2):
        for at, name in enumerate("huv"):
            start = (row * 3 + at) * 8
            edges[start : start + 8, :] = lax.dot_general(
                picker, state[name, row].astype(BF16), NT, preferred_element_type=F32
            )

    lane = lax.broadcasted_iota(jnp.int32, (members, lanes), 1)
    first = lane == 0
    last = lane == lanes - 1
    zero = jnp.zeros((members, lanes), F32)

    def span(value, halo):
        ahead = jnp.where(last, halo, pltpu.roll(value, lanes - 1, 1))
        behind = jnp.where(first, halo, pltpu.roll(value, 1, 1))
        return ahead - behind

    rows = lat * 2 + lax.broadcasted_iota(jnp.int32, (8, lanes), 0)
    latitude = BAND * (2.0 * (rows.astype(F32) + 0.5) / (2 * n_lat) - 1.0)
    rotation = ROTATION * jnp.sin(latitude)
    rot = [rotation[row : row + 1, :] for row in range(2)]

    @pl.when(jnp.logical_not(has_low))
    def _():
        from_low[...] = jnp.zeros_like(from_low)
        cols[96:128, :] = jnp.zeros((32, members), F32)

    @pl.when(jnp.logical_not(has_high))
    def _():
        from_high[...] = jnp.zeros_like(from_high)
        cols[128:160, :] = jnp.zeros((32, members), F32)

    pl.semaphore_wait(barrier, total - 1)

    def copy(source, target, at, to):
        return pltpu.make_async_remote_copy(
            src_ref=source, dst_ref=target, send_sem=send_sem.at[at], recv_sem=recv_sem.at[at],
            device_id=to, device_id_type=MESH,
        )

    def rows_of(buf, start, count):
        return buf.at[pl.ds(start, count)]

    lon_copies = [
        copy(edges, rows_of(cols, 48, 48), 0, (lat, west)),
        copy(edges, rows_of(cols, 0, 48), 1, (lat, east)),
    ]
    low = lat - 1
    high = lat + 1
    low_copies = [
        copy(rows_of(own, 0, 2), rows_of(from_high, 0, 2), 2, (low, lon)),
        copy(down_buf, rows_of(from_high, 2, 2), 3, (low, lon)),
        copy(rows_of(edges, 8, 16), rows_of(cols, 144, 16), 4, (low, west)),
        copy(rows_of(edges, 8, 16), rows_of(cols, 128, 16), 5, (low, east)),
    ]
    high_copies = [
        copy(rows_of(own, 3, 2), rows_of(from_low, 0, 2), 6, (high, lon)),
        copy(up_buf, rows_of(from_low, 2, 2), 7, (high, lon)),
        copy(rows_of(edges, 32, 16), rows_of(cols, 112, 16), 8, (high, west)),
        copy(rows_of(edges, 32, 16), rows_of(cols, 96, 16), 9, (high, east)),
    ]

    for item in lon_copies:
        item.start()

    @pl.when(has_high)
    def _():
        for at in (2, 3, 0):
            high_copies[at].start()

    @pl.when(has_low)
    def _():
        for at in (2, 3, 0):
            low_copies[at].start()

    h0, u0, v0 = (state[name, 0] for name in "huv")
    h1, u1, v1 = (state[name, 1] for name in "huv")
    c = HALF_COURANT
    up_buf[0] = h1 - c * span(u1, zero) + c * v0
    up_buf[1] = v1 + c * h0 - rot[1] * u1
    down_buf[0] = h0 - c * span(u0, zero) - c * v1
    down_buf[1] = v0 - c * h1 - rot[0] * u0

    @pl.when(has_high)
    def _():
        high_copies[1].start()

    @pl.when(has_low)
    def _():
        low_copies[1].start()

    for item in fetches[1:]:
        item.wait()
    slots = observed.shape[1]
    slot = lax.broadcasted_iota(jnp.int32, (1, slots), 1)
    live = jnp.where(slot < obs_count[0, 0], 1.0, 0.0)
    scale = live / obs_error[...]
    squared = scale * scale
    pieces = split3(squared) + split3(squared * observed[...])
    pieces = jnp.concatenate(pieces + (jnp.zeros((2, slots), F32),), axis=0).astype(BF16)
    cells = 6 * lanes
    cell = lax.broadcasted_iota(jnp.int32, (cells, slots), 0)
    hits = jnp.where(cell == obs_index[...], 1.0, 0.0).astype(BF16)
    sums = lax.dot_general(pieces, hits, NT, preferred_element_type=F32)
    weight = sums[0:1] + sums[1:2] + sums[2:3]
    target = sums[3:4] + sums[4:5] + sums[5:6]

    for item in lon_copies:
        item.wait()

    @pl.when(has_high)
    def _():
        for item in low_copies[2:]:
            item.wait_recv()

    @pl.when(has_low)
    def _():
        for item in high_copies[2:]:
            item.wait_recv()

    ahead_t = cols[...].astype(BF16)
    key = lax.broadcasted_iota(jnp.int32, (160, lanes), 0)
    spot = lax.broadcasted_iota(jnp.int32, (160, lanes), 1)

    def halo(west_at, east_at):
        chosen = jnp.where(
            ((key == west_at) & (spot == 0)) | ((key == east_at) & (spot == lanes - 1)), 1.0, 0.0
        ).astype(BF16)
        return lax.dot_general(ahead_t, chosen, TN, preferred_element_type=F32)

    def near(name, row):
        if 0 <= row < 2:
            at = (row * 3 + "huv".index(name)) * 8
            return halo(at + 3, 48 + at)
        base = 96 if row < 0 else 128
        at = base + "uv".index(name) * 8
        return halo(at + 3, at + 16)

    def far(name, row):
        at = (row * 3 + "huv".index(name)) * 8
        return halo(at + 2, 48 + at + 1)

    side = jnp.where(first, -1.0, jnp.where(last, 1.0, 0.0))
    inside_low = jnp.where(has_low, 1.0, 0.0)
    inside_high = jnp.where(has_high, 1.0, 0.0)

    mid_h = {
        -1: -c * side * near("u", -1) - (c * inside_low) * v0,
        2: -c * side * near("u", 2) + (c * inside_high) * v1,
    }
    mid_v = {-1: -(c * inside_low) * h0, 2: (c * inside_high) * h1}
    h = {-1: zero, 0: h0, 1: h1, 2: zero}
    v = {-1: zero, 0: v0, 1: v1, 2: zero}
    u = {0: u0, 1: u1}
    near_v = {row: near("v", row) for row in range(-1, 3)}
    rate = {}
    mid_u = {}
    edge_h = {}
    edge_u = {}
    for row in range(2):
        near_u = near("u", row)
        near_h = near("h", row)
        rate["h", row] = -c * (span(u[row], near_u) + (v[row + 1] - v[row - 1]))
        rate["u", row] = -c * span(h[row], near_h) + rot[row] * v[row]
        rate["v", row] = -c * (h[row + 1] - h[row - 1]) - rot[row] * u[row]
        mid_h[row] = h[row] + rate["h", row]
        mid_u[row] = u[row] + rate["u", row]
        mid_v[row] = v[row] + rate["v", row]
        edge_h[row] = near_h - c * (
            side * (far("u", row) - u[row]) + (near_v[row + 1] - near_v[row - 1])
        )
        edge_u[row] = near_u - c * side * (far("h", row) - h[row]) + rot[row] * near_v[row]

    for at, name in enumerate("huv"):
        for row in range(2):
            if name == "h":
                second = -c * (span(mid_u[row], edge_u[row]) + (mid_v[row + 1] - mid_v[row - 1]))
            elif name == "u":
                second = -c * span(mid_h[row], edge_h[row]) + rot[row] * mid_v[row]
            else:
                second = -c * (mid_h[row + 1] - mid_h[row - 1]) - rot[row] * mid_u[row]
            value = state[name, row] + 0.5 * (rate[name, row] + second)
            wide[pl.ds((at * 2 + row) * members, members), :] = value

    @pl.when(has_high)
    def _():
        for item in high_copies:
            item.wait_send()
        for item in low_copies[:2]:
            item.wait_recv()

    @pl.when(has_low)
    def _():
        for item in low_copies:
            item.wait_send()
        for item in high_copies[:2]:
            item.wait_recv()

    hm, vm, pm, qm = (from_low[at] for at in range(4))
    hp, vp, pp, qp = (from_high[at] for at in range(4))
    half = 0.5 * c
    more = {
        ("h", 0): half * (vm + qm + c * hp),
        ("h", 1): half * (c * hm - vp - qp),
        ("u", 0): half * (rot[0] * hm - c * span(vm, zero)),
        ("u", 1): half * (c * span(vp, zero) - rot[1] * hp),
        ("v", 0): half * (hm + pm + c * vp),
        ("v", 1): half * (c * vm - hp - pp),
    }
    for at, name in enumerate("huv"):
        for row in range(2):
            value = wide[pl.ds((at * 2 + row) * members, members), :] + more[name, row]
            center = jnp.sum(value, axis=0, keepdims=True) * (1.0 / members)
            block = slice((at * 2 + row) * lanes, (at * 2 + row + 1) * lanes)
            fields_out[0:members, block] = value - center
            fields_out[members : members + 8, block] = jnp.broadcast_to(center, (8, lanes))

    anomaly = fields_out[0:members, :]
    center = fields_out[members : members + 1, :]
    bottom = jnp.broadcast_to(target - weight * center, (8, cells))
    left = jnp.concatenate([anomaly * weight, bottom], axis=0)
    local = lax.dot_general(left, anomaly, NT, precision=HIGHEST, preferred_element_type=F32)
    for chunk in range(chunks):
        part[chunk] = local[chunk * 8 : chunk * 8 + 8, :]

    def part_copy(chunk):
        target_device = owner(chunk)
        distance = lax.rem(me - target_device + total, total)
        return pltpu.make_async_remote_copy(
            src_ref=part.at[chunk], dst_ref=gathered.at[distance - 1],
            send_sem=part_send.at[chunk], recv_sem=part_recv,
            device_id=place(target_device), device_id_type=MESH,
        )

    for chunk in range(chunks):
        @pl.when(owner(chunk) != me)
        def _():
            part_copy(chunk).start()

    def whole_copy(chunk, to):
        return pltpu.make_async_remote_copy(
            src_ref=whole.at[chunk], dst_ref=whole.at[chunk],
            send_sem=whole_send, recv_sem=whole_recv.at[chunk],
            device_id=to, device_id_type=MESH,
        )

    mine = [owner(chunk) == me for chunk in range(chunks)]
    my_chunk = sum(jnp.where(mine[chunk], chunk, 0) for chunk in range(chunks))
    owns = functools.reduce(jnp.logical_or, mine)

    @pl.when(owns)
    def _():
        pltpu.make_async_copy(gathered, gathered, part_recv).wait()
        whole[my_chunk] = part[my_chunk] + jnp.sum(gathered[...], axis=0)

        def send_lat(step, start):
            to_lat = lax.rem(lat + step, n_lat)
            to_lon = lax.rem(lon + start, n_lon)
            for _ in range(start, n_lon):
                whole_copy(my_chunk, (to_lat, to_lon)).start()
                to_lon = jnp.where(to_lon == n_lon - 1, 0, to_lon + 1)

        def send(step, carry):
            send_lat(step, 0)
            return carry

        lax.fori_loop(1, n_lat, send, 0)
        send_lat(0, 1)

    for chunk in range(chunks):
        @pl.when(owner(chunk) != me)
        def _():
            part_copy(chunk).wait_send()
            whole_copy(chunk, (lat, east)).wait_recv()

    for chunk in range(chunks):
        total_out[chunk * 8 : chunk * 8 + 8, :] = whole[chunk]

    @pl.when(owns)
    def _():
        pltpu.make_async_copy(gathered, gathered, whole_send).wait()


def update_kernel(fields, sums, out, work, inverse):
    members = work.shape[0]
    lanes = out.shape[1]
    prior = float(members - 1)
    row = lax.broadcasted_iota(jnp.int32, (members, members), 0)
    col = lax.broadcasted_iota(jnp.int32, (members, members), 1)
    work[...] = sums[0:members, :] + jnp.where(row == col, prior, 0.0)
    sub = lax.broadcasted_iota(jnp.int32, (PANEL, members), 0)
    at = lax.broadcasted_iota(jnp.int32, (PANEL, members), 1)
    for start in range(0, members, PANEL):
        stop = start + PANEL
        panel = work[start:stop, :]
        columns = [
            jnp.broadcast_to(panel[:, start + k : start + k + 1], (PANEL, members))
            for k in range(PANEL)
        ]
        reciprocal = jnp.zeros((PANEL, members), F32)
        for k in range(PANEL):
            over = 1.0 / columns[k][k : k + 1, :]
            reciprocal = jnp.where(sub == k, over, reciprocal)
            below = jnp.where(sub > k, columns[k], 0.0)
            panel = jnp.where(
                at == start + k, jnp.where(sub == k, 1.0, jnp.where(sub > k, 0.0, panel)), panel
            )
            panel = panel - (below * panel[k : k + 1, :]) * over
            for j in range(k + 1, PANEL):
                columns[j] = columns[j] - (below * columns[j][k : k + 1, :]) * over
        inverse[start:stop, :] = jnp.where(at <= start + sub, panel, 0.0) * jnp.sqrt(reciprocal)
        if stop < members:
            ratios = panel * reciprocal
            used = jnp.where((at > start + sub) & (at < stop), 0.0, panel)
            change = lax.dot_general(
                ratios, used, TN, precision=HIGHEST, preferred_element_type=F32
            )
            below = work[stop:, :]
            keep = (col[stop:, :] < start) | (col[stop:, :] >= stop)
            work[stop:, :] = jnp.where(keep, below, 0.0) - change[stop:, :]
    lower = inverse[...]
    push = sums[members : members + 8, :]
    forward = lax.dot_general(push, lower, NT, precision=HIGHEST, preferred_element_type=F32)
    mean_weights = jnp.dot(forward, lower, precision=HIGHEST, preferred_element_type=F32)
    weights = math.sqrt(prior) * lower + mean_weights[0:1, :]
    anomaly = fields[0:members, :]
    center = fields[members : members + 1, :]
    result = center + jnp.dot(weights, anomaly, precision=HIGHEST, preferred_element_type=F32)
    for block in range(6):
        field, line = block // 2, block % 2
        out[pl.ds(field * 2 * members + line, members, stride=2), :] = result[
            :, block * lanes : (block + 1) * lanes
        ]


def shards(n_lat, n_lon, prior_ensemble, observed, obs_error, obs_index, obs_count):
    fields, members, rows, lanes = prior_ensemble.shape
    cells = fields * rows * lanes
    total = n_lat * n_lon
    chunks = members // 8 + 1
    vmem = pl.BlockSpec(memory_space=pltpu.VMEM)
    slots = observed.shape[-1]
    forecast, sums = pl.pallas_call(
        functools.partial(forecast_kernel, n_lat, n_lon),
        out_shape=(
            jax.ShapeDtypeStruct((members + 8, cells), F32),
            jax.ShapeDtypeStruct((members + 8, members), F32),
        ),
        in_specs=[pl.BlockSpec(memory_space=pl.ANY)] * 5,
        out_specs=(vmem, vmem),
        scratch_shapes=[
            pltpu.VMEM((fields * members * rows, lanes), prior_ensemble.dtype),
            pltpu.VMEM((1, slots), F32),
            pltpu.VMEM((1, slots), F32),
            pltpu.VMEM((1, slots), jnp.int32),
            pltpu.SMEM((1, 1), jnp.int32),
            pltpu.SemaphoreType.DMA((5,)),
            pltpu.VMEM((fields * members * rows, lanes), F32),
            pltpu.VMEM((6, members, lanes), F32),
            pltpu.VMEM((2, members, lanes), F32),
            pltpu.VMEM((2, members, lanes), F32),
            pltpu.VMEM((48, members), F32),
            pltpu.VMEM((4, members, lanes), F32),
            pltpu.VMEM((4, members, lanes), F32),
            pltpu.VMEM((160, members), F32),
            pltpu.VMEM((chunks, 8, members), F32),
            pltpu.VMEM((total - 1, 8, members), F32),
            pltpu.VMEM((chunks, 8, members), F32),
            pltpu.SemaphoreType.DMA((10,)),
            pltpu.SemaphoreType.DMA((10,)),
            pltpu.SemaphoreType.DMA((chunks,)),
            pltpu.SemaphoreType.DMA,
            pltpu.SemaphoreType.DMA,
            pltpu.SemaphoreType.DMA((chunks,)),
        ],
        compiler_params=pltpu.CompilerParams(
            collective_id=0, has_side_effects=True, vmem_limit_bytes=VMEM_LIMIT
        ),
    )(
        prior_ensemble.reshape(-1, lanes), observed.reshape(1, slots), obs_error.reshape(1, slots),
        obs_index.reshape(1, slots), obs_count,
    )
    out = pl.pallas_call(
        update_kernel,
        out_shape=jax.ShapeDtypeStruct((fields * members * rows, lanes), F32),
        in_specs=[vmem, vmem],
        out_specs=vmem,
        scratch_shapes=[
            pltpu.VMEM((members, members), F32),
            pltpu.VMEM((members, members), F32),
        ],
        compiler_params=pltpu.CompilerParams(vmem_limit_bytes=VMEM_LIMIT),
    )(forecast, sums)
    return out.reshape(prior_ensemble.shape)


def solution(mesh):
    placed = (
        P(None, None, "lat", "lon"),
        P("lat", "lon", None),
        P("lat", "lon", None),
        P("lat", "lon", None),
        P("lat", "lon"),
    )
    return jax.shard_map(
        functools.partial(shards, mesh.shape["lat"], mesh.shape["lon"]),
        mesh=mesh, in_specs=placed, out_specs=P(None, None, "lat", "lon"), check_vma=False,
    )
```

```python
import functools
import math

import jax
import jax.numpy as jnp
from jax import lax
from jax.experimental import pallas as pl
from jax.experimental.pallas import tpu as pltpu
from jax.sharding import PartitionSpec as P

HALF_COURANT = 0.4
ROTATION = 0.8
BAND = math.pi / 6.0
MESH = pl.DeviceIdType.MESH
F32 = jnp.float32
BF16 = jnp.bfloat16
HIGHEST = lax.Precision.HIGHEST
NT = (((1,), (1,)), ((), ()))
TN = (((0,), (0,)), ((), ()))
PANEL = 32
VMEM_LIMIT = 56 * 1024 * 1024


def split3(value):
    high = value.astype(BF16).astype(F32)
    rest = value - high
    middle = rest.astype(BF16).astype(F32)
    return high, middle, rest - middle


def forecast_kernel(
    n_lat, n_lon, prior_in, observed_in, obs_error_in, obs_index_in, count_in,
    fields_hbm, center_hbm, total_out,
    fields, centers, gram_left, out_sem, prior, observed, obs_error, obs_index, obs_count, in_sem,
    wide, own, up_buf, down_buf, edges, from_low, from_high, cols, part, gathered, whole,
    send_sem, recv_sem, part_send, part_recv, whole_send, whole_recv,
):
    members = own.shape[1]
    lanes = own.shape[2]
    total = n_lat * n_lon
    lat = lax.axis_index("lat")
    lon = lax.axis_index("lon")
    me = lat * n_lon + lon
    east = lax.rem(lon + 1, n_lon)
    west = lax.rem(lon + n_lon - 1, n_lon)
    has_low = lat > 0
    has_high = lat < n_lat - 1
    chunks = part.shape[0]

    def place(index):
        return (index // n_lon, lax.rem(index, n_lon))

    def owner(chunk):
        line = 2 * (chunk // n_lon)
        return (line % n_lat + line // n_lat) * n_lon + chunk % n_lon

    fetches = [
        pltpu.make_async_copy(source, target, in_sem.at[at])
        for at, (source, target) in enumerate(
            (
                (prior_in, prior), (observed_in, observed), (obs_error_in, obs_error),
                (obs_index_in, obs_index), (count_in, obs_count),
            )
        )
    ]
    for item in fetches:
        item.start()
    barrier = pltpu.get_barrier_semaphore()

    def greet(step, carry):
        pl.semaphore_signal(
            barrier, inc=1, device_id=place(lax.rem(me + step, total)), device_id_type=MESH
        )
        return carry

    lax.fori_loop(1, total, greet, 0)
    fetches[0].wait()

    wide[...] = prior[...].astype(F32)
    field_at = {"h": 0, "u": 1, "v": 2}
    slot_of = {"h": 0, "v": 1, "u": 2}
    state = {}
    for row in range(2):
        for name in "huv":
            block = wide[pl.ds(field_at[name] * 2 * members + row, members, stride=2), :]
            state[name, row] = block
            own[row * 3 + slot_of[name]] = block

    pick_row = lax.broadcasted_iota(jnp.int32, (8, lanes), 0)
    pick_col = lax.broadcasted_iota(jnp.int32, (8, lanes), 1)
    wanted = jnp.where(pick_row < 2, pick_row, pick_row + (lanes - 4))
    picker = jnp.where((pick_col == wanted) & (pick_row < 4), 1.0, 0.0).astype(BF16)
    for row in range(2):
        for at, name in enumerate("huv"):
            start = (row * 3 + at) * 8
            edges[start : start + 8, :] = lax.dot_general(
                picker, state[name, row].astype(BF16), NT, preferred_element_type=F32
            )

    lane = lax.broadcasted_iota(jnp.int32, (members, lanes), 1)
    first = lane == 0
    last = lane == lanes - 1
    zero = jnp.zeros((members, lanes), F32)

    def span(value, halo):
        ahead = jnp.where(last, halo, pltpu.roll(value, lanes - 1, 1))
        behind = jnp.where(first, halo, pltpu.roll(value, 1, 1))
        return ahead - behind

    rows = lat * 2 + lax.broadcasted_iota(jnp.int32, (8, lanes), 0)
    latitude = BAND * (2.0 * (rows.astype(F32) + 0.5) / (2 * n_lat) - 1.0)
    rotation = ROTATION * jnp.sin(latitude)
    rot = [rotation[row : row + 1, :] for row in range(2)]

    @pl.when(jnp.logical_not(has_low))
    def _():
        from_low[...] = jnp.zeros_like(from_low)
        cols[96:128, :] = jnp.zeros((32, members), F32)

    @pl.when(jnp.logical_not(has_high))
    def _():
        from_high[...] = jnp.zeros_like(from_high)
        cols[128:160, :] = jnp.zeros((32, members), F32)

    pl.semaphore_wait(barrier, total - 1)

    def copy(source, target, at, to):
        return pltpu.make_async_remote_copy(
            src_ref=source, dst_ref=target, send_sem=send_sem.at[at], recv_sem=recv_sem.at[at],
            device_id=to, device_id_type=MESH,
        )

    def rows_of(buf, start, count):
        return buf.at[pl.ds(start, count)]

    lon_copies = [
        copy(edges, rows_of(cols, 48, 48), 0, (lat, west)),
        copy(edges, rows_of(cols, 0, 48), 1, (lat, east)),
    ]
    low = lat - 1
    high = lat + 1
    low_copies = [
        copy(rows_of(own, 0, 2), rows_of(from_high, 0, 2), 2, (low, lon)),
        copy(down_buf, rows_of(from_high, 2, 2), 3, (low, lon)),
        copy(rows_of(edges, 8, 16), rows_of(cols, 144, 16), 4, (low, west)),
        copy(rows_of(edges, 8, 16), rows_of(cols, 128, 16), 5, (low, east)),
    ]
    high_copies = [
        copy(rows_of(own, 3, 2), rows_of(from_low, 0, 2), 6, (high, lon)),
        copy(up_buf, rows_of(from_low, 2, 2), 7, (high, lon)),
        copy(rows_of(edges, 32, 16), rows_of(cols, 112, 16), 8, (high, west)),
        copy(rows_of(edges, 32, 16), rows_of(cols, 96, 16), 9, (high, east)),
    ]

    for item in lon_copies:
        item.start()

    @pl.when(has_high)
    def _():
        for at in (2, 3, 0):
            high_copies[at].start()

    @pl.when(has_low)
    def _():
        for at in (2, 3, 0):
            low_copies[at].start()

    h0, u0, v0 = (state[name, 0] for name in "huv")
    h1, u1, v1 = (state[name, 1] for name in "huv")
    c = HALF_COURANT
    up_buf[0] = h1 - c * span(u1, zero) + c * v0
    up_buf[1] = v1 + c * h0 - rot[1] * u1
    down_buf[0] = h0 - c * span(u0, zero) - c * v1
    down_buf[1] = v0 - c * h1 - rot[0] * u0

    @pl.when(has_high)
    def _():
        high_copies[1].start()

    @pl.when(has_low)
    def _():
        low_copies[1].start()

    for item in fetches[1:]:
        item.wait()
    slots = observed.shape[1]
    slot = lax.broadcasted_iota(jnp.int32, (1, slots), 1)
    live = jnp.where(slot < obs_count[0, 0], 1.0, 0.0)
    scale = live / obs_error[...]
    squared = scale * scale
    pieces = split3(squared) + split3(squared * observed[...])
    pieces = jnp.concatenate(pieces + (jnp.zeros((2, slots), F32),), axis=0).astype(BF16)
    cells = 6 * lanes
    cell = lax.broadcasted_iota(jnp.int32, (cells, slots), 0)
    hits = jnp.where(cell == obs_index[...], 1.0, 0.0).astype(BF16)
    sums = lax.dot_general(pieces, hits, NT, preferred_element_type=F32)
    weight = sums[0:1] + sums[1:2] + sums[2:3]
    target = sums[3:4] + sums[4:5] + sums[5:6]

    for item in lon_copies:
        item.wait()

    @pl.when(has_high)
    def _():
        for item in low_copies[2:]:
            item.wait_recv()

    @pl.when(has_low)
    def _():
        for item in high_copies[2:]:
            item.wait_recv()

    ahead = cols[...].T.astype(BF16)
    key = lax.broadcasted_iota(jnp.int32, (160, lanes), 0)
    spot = lax.broadcasted_iota(jnp.int32, (160, lanes), 1)

    def halo(west_at, east_at):
        chosen = jnp.where(
            ((key == west_at) & (spot == 0)) | ((key == east_at) & (spot == lanes - 1)), 1.0, 0.0
        ).astype(BF16)
        return jnp.dot(ahead, chosen, preferred_element_type=F32)

    def near(name, row):
        if 0 <= row < 2:
            at = (row * 3 + "huv".index(name)) * 8
            return halo(at + 3, 48 + at)
        base = 96 if row < 0 else 128
        at = base + "uv".index(name) * 8
        return halo(at + 3, at + 16)

    def far(name, row):
        at = (row * 3 + "huv".index(name)) * 8
        return halo(at + 2, 48 + at + 1)

    side = jnp.where(first, -1.0, jnp.where(last, 1.0, 0.0))
    inside_low = jnp.where(has_low, 1.0, 0.0)
    inside_high = jnp.where(has_high, 1.0, 0.0)

    mid_h = {
        -1: -c * side * near("u", -1) - (c * inside_low) * v0,
        2: -c * side * near("u", 2) + (c * inside_high) * v1,
    }
    mid_v = {-1: -(c * inside_low) * h0, 2: (c * inside_high) * h1}
    h = {-1: zero, 0: h0, 1: h1, 2: zero}
    v = {-1: zero, 0: v0, 1: v1, 2: zero}
    u = {0: u0, 1: u1}
    near_v = {row: near("v", row) for row in range(-1, 3)}
    rate = {}
    mid_u = {}
    edge_h = {}
    edge_u = {}
    for row in range(2):
        near_u = near("u", row)
        near_h = near("h", row)
        rate["h", row] = -c * (span(u[row], near_u) + (v[row + 1] - v[row - 1]))
        rate["u", row] = -c * span(h[row], near_h) + rot[row] * v[row]
        rate["v", row] = -c * (h[row + 1] - h[row - 1]) - rot[row] * u[row]
        mid_h[row] = h[row] + rate["h", row]
        mid_u[row] = u[row] + rate["u", row]
        mid_v[row] = v[row] + rate["v", row]
        edge_h[row] = near_h - c * (
            side * (far("u", row) - u[row]) + (near_v[row + 1] - near_v[row - 1])
        )
        edge_u[row] = near_u - c * side * (far("h", row) - h[row]) + rot[row] * near_v[row]

    for at, name in enumerate("huv"):
        for row in range(2):
            if name == "h":
                second = -c * (span(mid_u[row], edge_u[row]) + (mid_v[row + 1] - mid_v[row - 1]))
            elif name == "u":
                second = -c * span(mid_h[row], edge_h[row]) + rot[row] * mid_v[row]
            else:
                second = -c * (mid_h[row + 1] - mid_h[row - 1]) - rot[row] * mid_u[row]
            value = state[name, row] + 0.5 * (rate[name, row] + second)
            wide[pl.ds((at * 2 + row) * members, members), :] = value

    @pl.when(has_high)
    def _():
        for item in high_copies:
            item.wait_send()
        for item in low_copies[:2]:
            item.wait_recv()

    @pl.when(has_low)
    def _():
        for item in low_copies:
            item.wait_send()
        for item in high_copies[:2]:
            item.wait_recv()

    hm, vm, pm, qm = (from_low[at] for at in range(4))
    hp, vp, pp, qp = (from_high[at] for at in range(4))
    half = 0.5 * c
    more = {
        ("h", 0): half * (vm + qm + c * hp),
        ("h", 1): half * (c * hm - vp - qp),
        ("u", 0): half * (rot[0] * hm - c * span(vm, zero)),
        ("u", 1): half * (c * span(vp, zero) - rot[1] * hp),
        ("v", 0): half * (hm + pm + c * vp),
        ("v", 1): half * (c * vm - hp - pp),
    }
    for at, name in enumerate("huv"):
        for row in range(2):
            value = wide[pl.ds((at * 2 + row) * members, members), :] + more[name, row]
            center = jnp.sum(value, axis=0, keepdims=True) * (1.0 / members)
            block = slice((at * 2 + row) * lanes, (at * 2 + row + 1) * lanes)
            anomaly = value - center
            above = anomaly.astype(BF16)
            fields[0:members, block] = above
            fields[members:, block] = (anomaly - above.astype(F32)).astype(BF16)
            centers[:, block] = jnp.broadcast_to(center, (8, lanes))
            share = weight[:, block]
            scaled = jnp.concatenate(
                [
                    anomaly * share,
                    jnp.broadcast_to(target[:, block] - share * center, (16, lanes)),
                ],
                axis=0,
            )
            above = scaled.astype(BF16)
            gram_left[0, :, block] = above
            gram_left[1, :, block] = (scaled - above.astype(F32)).astype(BF16)

    fields_copy = pltpu.make_async_copy(fields, fields_hbm, out_sem.at[0])
    center_copy = pltpu.make_async_copy(centers, center_hbm, out_sem.at[1])
    fields_copy.start()
    center_copy.start()

    def product(left, right):
        return lax.dot_general(left, right, NT, preferred_element_type=F32)

    local = product(gram_left[0], fields[0:members, :])
    local += product(gram_left[0], fields[members:, :])
    local += product(gram_left[1], fields[0:members, :])
    for chunk in range(chunks):
        part[chunk] = local[chunk * 8 : chunk * 8 + 8, :]

    def part_copy(chunk):
        target_device = owner(chunk)
        distance = lax.rem(me - target_device + total, total)
        return pltpu.make_async_remote_copy(
            src_ref=part.at[chunk], dst_ref=gathered.at[distance - 1],
            send_sem=part_send.at[chunk], recv_sem=part_recv,
            device_id=place(target_device), device_id_type=MESH,
        )

    for chunk in range(chunks):
        @pl.when(owner(chunk) != me)
        def _():
            part_copy(chunk).start()

    def whole_copy(chunk, to):
        return pltpu.make_async_remote_copy(
            src_ref=whole.at[chunk], dst_ref=whole.at[chunk],
            send_sem=whole_send, recv_sem=whole_recv.at[chunk],
            device_id=to, device_id_type=MESH,
        )

    mine = [owner(chunk) == me for chunk in range(chunks)]
    my_chunk = sum(jnp.where(mine[chunk], chunk, 0) for chunk in range(chunks))
    owns = functools.reduce(jnp.logical_or, mine)

    @pl.when(owns)
    def _():
        pltpu.make_async_copy(gathered, gathered, part_recv).wait()
        whole[my_chunk] = part[my_chunk] + jnp.sum(gathered[...], axis=0)

        def send_lat(step, start):
            to_lat = lax.rem(lat + step, n_lat)
            to_lon = lax.rem(lon + start, n_lon)
            for _ in range(start, n_lon):
                whole_copy(my_chunk, (to_lat, to_lon)).start()
                to_lon = jnp.where(to_lon == n_lon - 1, 0, to_lon + 1)

        def send(step, carry):
            send_lat(step, 0)
            return carry

        lax.fori_loop(1, n_lat, send, 0)
        send_lat(0, 1)

    for chunk in range(chunks):
        @pl.when(owner(chunk) != me)
        def _():
            part_copy(chunk).wait_send()
            whole_copy(chunk, (lat, east)).wait_recv()

    for chunk in range(chunks):
        total_out[chunk * 8 : chunk * 8 + 8, :] = whole[chunk]

    @pl.when(owns)
    def _():
        pltpu.make_async_copy(gathered, gathered, whole_send).wait()

    fields_copy.wait()
    center_copy.wait()


def inverse_of(pivot):
    guess = pl.reciprocal(pivot, approx=True)
    guess = guess * (2.0 - pivot * guess)
    return guess * (2.0 - pivot * guess)


def update_kernel(
    fields_hbm, center_hbm, sums, out_hbm, fields, centers, out, work, inverse, in_sem, out_sem
):
    fetches = [
        pltpu.make_async_copy(fields_hbm, fields, in_sem.at[0]),
        pltpu.make_async_copy(center_hbm, centers, in_sem.at[1]),
    ]
    for item in fetches:
        item.start()
    members = work.shape[0]
    lanes = out.shape[1]
    prior = float(members - 1)
    row = lax.broadcasted_iota(jnp.int32, (members, members), 0)
    col = lax.broadcasted_iota(jnp.int32, (members, members), 1)
    work[...] = sums[0:members, :] + jnp.where(row == col, prior, 0.0)
    sub = lax.broadcasted_iota(jnp.int32, (8, members), 0)
    at = lax.broadcasted_iota(jnp.int32, (8, members), 1)
    groups = PANEL // 8
    for start in range(0, members, PANEL):
        stop = start + PANEL
        panel = [work[start + 8 * g : start + 8 * g + 8, :] for g in range(groups)]
        columns = {
            (g, k): jnp.broadcast_to(panel[g][:, start + k : start + k + 1], (8, members))
            for g in range(groups)
            for k in range(PANEL)
        }
        reciprocal = [jnp.zeros((8, members), F32) for _ in range(groups)]
        for k in range(PANEL):
            own, line = k // 8, k % 8
            over = inverse_of(columns[own, k][line : line + 1, :])
            reciprocal[own] = jnp.where(sub == line, over, reciprocal[own])
            here = at == start + k
            pivot = jnp.where(here[0:1, :], 1.0, panel[own][line : line + 1, :])
            factors = {j: columns[own, j][line : line + 1, :] for j in range(k + 1, PANEL)}
            for g in range(own, groups):
                below = columns[g, k]
                if g == own:
                    below = jnp.where(sub > line, below, 0.0)
                    cleared = jnp.where(
                        here, jnp.where(sub == line, 1.0, jnp.where(sub > line, 0.0, panel[g])), panel[g]
                    )
                else:
                    cleared = jnp.where(here, 0.0, panel[g])
                panel[g] = cleared - (below * pivot) * over
                for j in range(k + 1, PANEL):
                    columns[g, j] = columns[g, j] - (below * factors[j]) * over
        for g in range(groups):
            inverse[start + 8 * g : start + 8 * g + 8, :] = jnp.where(
                at <= start + 8 * g + sub, panel[g], 0.0
            ) * jnp.sqrt(reciprocal[g])
        if stop < members:
            ratios = jnp.concatenate([panel[g] * reciprocal[g] for g in range(groups)], axis=0)
            used = jnp.concatenate(
                [
                    jnp.where((at > start + 8 * g + sub) & (at < stop), 0.0, panel[g])
                    for g in range(groups)
                ],
                axis=0,
            )
            change = lax.dot_general(
                ratios, used, TN, precision=HIGHEST, preferred_element_type=F32
            )
            below = work[stop:, :]
            keep = (col[stop:, :] < start) | (col[stop:, :] >= stop)
            work[stop:, :] = jnp.where(keep, below, 0.0) - change[stop:, :]
    lower = inverse[...]
    push = sums[members : members + 8, :]
    forward = lax.dot_general(push, lower, NT, precision=HIGHEST, preferred_element_type=F32)
    mean_weights = jnp.dot(forward, lower, precision=HIGHEST, preferred_element_type=F32)
    weights = math.sqrt(prior) * lower + mean_weights[0:1, :]
    above = weights.astype(BF16)
    rest = (weights - above.astype(F32)).astype(BF16)
    twice = jnp.concatenate([above, above], axis=1)
    for item in fetches:
        item.wait()
    copies = []
    for field in range(3):
        block = slice(field * 2 * lanes, (field + 1) * 2 * lanes)
        result = centers[0:1, block] + (
            jnp.dot(twice, fields[:, block], preferred_element_type=F32)
            + jnp.dot(rest, fields[0:members, block], preferred_element_type=F32)
        )
        for line in range(2):
            out[pl.ds(field * 2 * members + line, members, stride=2), :] = result[
                :, line * lanes : (line + 1) * lanes
            ]
        span = pl.ds(field * 2 * members, 2 * members)
        copies.append(pltpu.make_async_copy(out.at[span], out_hbm.at[span], out_sem.at[field]))
        copies[-1].start()
    for item in copies:
        item.wait()


def shards(n_lat, n_lon, prior_ensemble, observed, obs_error, obs_index, obs_count):
    fields, members, rows, lanes = prior_ensemble.shape
    cells = fields * rows * lanes
    total = n_lat * n_lon
    chunks = members // 8 + 1
    vmem = pl.BlockSpec(memory_space=pltpu.VMEM)
    slots = observed.shape[-1]
    hbm = pl.BlockSpec(memory_space=pl.ANY)
    forecast, center, sums = pl.pallas_call(
        functools.partial(forecast_kernel, n_lat, n_lon),
        out_shape=(
            jax.ShapeDtypeStruct((2 * members, cells), BF16),
            jax.ShapeDtypeStruct((8, cells), F32),
            jax.ShapeDtypeStruct((members + 8, members), F32),
        ),
        in_specs=[hbm] * 5,
        out_specs=(hbm, hbm, vmem),
        scratch_shapes=[
            pltpu.VMEM((2 * members, cells), BF16),
            pltpu.VMEM((8, cells), F32),
            pltpu.VMEM((2, members + 16, cells), BF16),
            pltpu.SemaphoreType.DMA((2,)),
            pltpu.VMEM((fields * members * rows, lanes), prior_ensemble.dtype),
            pltpu.VMEM((1, slots), F32),
            pltpu.VMEM((1, slots), F32),
            pltpu.VMEM((1, slots), jnp.int32),
            pltpu.SMEM((1, 1), jnp.int32),
            pltpu.SemaphoreType.DMA((5,)),
            pltpu.VMEM((fields * members * rows, lanes), F32),
            pltpu.VMEM((6, members, lanes), F32),
            pltpu.VMEM((2, members, lanes), F32),
            pltpu.VMEM((2, members, lanes), F32),
            pltpu.VMEM((48, members), F32),
            pltpu.VMEM((4, members, lanes), F32),
            pltpu.VMEM((4, members, lanes), F32),
            pltpu.VMEM((160, members), F32),
            pltpu.VMEM((chunks, 8, members), F32),
            pltpu.VMEM((total - 1, 8, members), F32),
            pltpu.VMEM((chunks, 8, members), F32),
            pltpu.SemaphoreType.DMA((10,)),
            pltpu.SemaphoreType.DMA((10,)),
            pltpu.SemaphoreType.DMA((chunks,)),
            pltpu.SemaphoreType.DMA,
            pltpu.SemaphoreType.DMA,
            pltpu.SemaphoreType.DMA((chunks,)),
        ],
        compiler_params=pltpu.CompilerParams(
            collective_id=0, has_side_effects=True, vmem_limit_bytes=VMEM_LIMIT
        ),
    )(
        prior_ensemble.reshape(-1, lanes), observed.reshape(1, slots), obs_error.reshape(1, slots),
        obs_index.reshape(1, slots), obs_count,
    )
    out = pl.pallas_call(
        update_kernel,
        out_shape=jax.ShapeDtypeStruct((fields * members * rows, lanes), F32),
        in_specs=[hbm, hbm, vmem],
        out_specs=hbm,
        scratch_shapes=[
            pltpu.VMEM((2 * members, cells), BF16),
            pltpu.VMEM((8, cells), F32),
            pltpu.VMEM((fields * members * rows, lanes), F32),
            pltpu.VMEM((members, members), F32),
            pltpu.VMEM((members, members), F32),
            pltpu.SemaphoreType.DMA((2,)),
            pltpu.SemaphoreType.DMA((3,)),
        ],
        compiler_params=pltpu.CompilerParams(vmem_limit_bytes=VMEM_LIMIT),
    )(forecast, center, sums)
    return out.reshape(prior_ensemble.shape)


def solution(mesh):
    placed = (
        P(None, None, "lat", "lon"),
        P("lat", "lon", None),
        P("lat", "lon", None),
        P("lat", "lon", None),
        P("lat", "lon"),
    )
    return jax.shard_map(
        functools.partial(shards, mesh.shape["lat"], mesh.shape["lon"]),
        mesh=mesh, in_specs=placed, out_specs=P(None, None, "lat", "lon"), check_vma=False,
    )
```
